128 devices in a mesh: freq: 4 (over z), space: 32 (over x, y, core).
Axes of the slice: x: 4, y: 4, z: 4, core: 2. Of those that a mesh axis runs over, the one named last changes fastest.
Arguments:
- recorded: bfloat16 [8, 2, 8192, 128], P('freq', None, 'space'), may hold values from -6 to 6
- v_factors: bfloat16 [8, 32, 2, 8192, 128], P('freq', None, None, 'space'), may hold values from -0.25 to 0.25
- u_factors: bfloat16 [8, 2, 8192, 32, 128], P('freq', None, 'space'), may hold values from -0.125 to 0.125
- tile_ranks: int32 [8, 32, 32], P('freq'), may hold values from 0 to 128, as said below
- mute_start: int32 [8192, 128], P('space', 'freq'), may hold values from 0 to 127
Outputs:
- muted_traces: float32 [8192, 128, 128], P('space', 'freq')
The draws below stay inside these ranges and needn't reach their ends.
Inputs may be any that keep to these rules, and one draw needn't show every extreme that they name: `tile_ranks`: entries with i equal to j are 128; every other entry is 0 or 64.
All inputs are finite; a program needn't handle non-finite values.
Results may differ from the reference program's by a relative error of at most 0.0041.
Values may be sent and summed in bfloat16 or wider, within the bound.
No kernel may reach another device: no remote copies, remote signals or barrier semaphores. Data moves between devices by JAX's collectives and lax.ppermute only.
A program may use at most 64 MiB of HBM per device.

```python
import math
import jax
import jax.numpy as jnp
from jax import lax

TILE = 256
RMAX = 128
NS = 128
NT = 128
F = 8
NTILE = 32
NR = 8192


def draw_tile_ranks(key, part):
    tile_count = NR // TILE
    rolled_values = jax.random.randint(key, (F, tile_count, tile_count), 0, 9)
    levels = jnp.where(rolled_values < 4, RMAX // 2, 0)
    lines = jnp.arange(tile_count, dtype=jnp.int32)
    diagonal = (lines[:, None] == lines[None, :])[None, :, :]
    return jnp.where(diagonal, RMAX, levels).astype(jnp.int32)


def with_ends(entries, rng, smallest, largest):
    longest = entries.shape.index(max(entries.shape))
    spots = []
    for shift in (0, 1):
        where = [jax.random.randint(jax.random.fold_in(rng, axis), (), 0, length) for axis, length in enumerate(entries.shape)]
        where[longest] = (where[longest] + shift) % entries.shape[longest]
        spots.append(tuple(where))
    return entries.at[spots[0]].set(smallest).at[spots[1]].set(largest)


def shard_levels(own_key, shape, shards, low, top_value):
    loudness = 1.0
    for position, parts in shards:
        steps = jax.random.uniform(jax.random.fold_in(jax.random.fold_in(own_key, 6), position), (parts,), jnp.float32, low / len(shards), top_value / len(shards))
        loudness = loudness * jnp.repeat(jnp.exp(steps), shape[position] // parts).reshape((-1,) + (1,) * (len(shape) - 1 - position))
    return loudness


def gaussian(rng, dims, scale, limit, cuts=(), kind=jnp.bfloat16):
    drawn = jax.random.normal(rng, dims, jnp.float32) * scale
    if len(cuts) > 0:
        drawn = shard_levels(rng, dims, cuts, -0.22, 0.18) * drawn
    return jnp.clip(drawn, min=-limit, max=limit).astype(kind)


def setup_inputs(seed: int = 0) -> dict:
    key_list = jax.random.split(jax.random.key(seed), 6)
    return {
        "recorded": gaussian(key_list[0], (F, 2, NR, NS), 1.0, 6.0, ((0, 4), (2, 32))),
        "v_factors": gaussian(key_list[1], (F, NTILE, 2, NR, RMAX), (2 * TILE) ** -0.5, 0.25, ((0, 4), (3, 32))),
        "u_factors": gaussian(key_list[2], (F, 2, NR, NTILE, RMAX), (2 * (RMAX + (NTILE - 1) * RMAX * 2 // 9)) ** -0.5, 0.125, ((0, 4), (2, 32))),
        "tile_ranks": draw_tile_ranks(jax.random.fold_in(key_list[5], 71), 0),
        "mute_start": with_ends(jax.random.randint(key_list[4], (NR, NS), 0, NT), jax.random.fold_in(key_list[4], 1), 0, NT - 1).astype(jnp.int32),
    }


def reference(recorded, v_factors, u_factors, tile_ranks, mute_start):
    tile_count = NR // TILE
    spectra_list = []
    for slot in range(F):
        data_freq = recorded[slot].astype(jnp.float32).reshape(2, tile_count, TILE, NS)
        v_freq = v_factors[slot].reshape(tile_count, 2, tile_count, TILE, RMAX)
        u_freq = jnp.moveaxis(u_factors[slot].reshape(2, tile_count, TILE, tile_count, RMAX), 1, 0)

        def one_row(row_items):
            v_row, u_row, rank_row = row_items
            v_row = v_row.astype(jnp.float32)
            u_row = u_row.astype(jnp.float32)
            high = lax.Precision.HIGHEST
            block_real = jnp.einsum('jqk,jqs->jks', v_row[0], data_freq[0], precision=high) - jnp.einsum('jqk,jqs->jks', v_row[1], data_freq[1], precision=high)
            block_imag = jnp.einsum('jqk,jqs->jks', v_row[0], data_freq[1], precision=high) + jnp.einsum('jqk,jqs->jks', v_row[1], data_freq[0], precision=high)
            kept = (jnp.arange(RMAX, dtype=jnp.int32)[None, :] < rank_row[:, None])[:, :, None]
            block_real = lax.optimization_barrier(jnp.where(kept, block_real, 0.0).astype(jnp.bfloat16)).astype(jnp.float32)
            block_imag = lax.optimization_barrier(jnp.where(kept, block_imag, 0.0).astype(jnp.bfloat16)).astype(jnp.float32)
            real_part = jnp.einsum('pjk,jks->ps', u_row[0], block_real, precision=high) - jnp.einsum('pjk,jks->ps', u_row[1], block_imag, precision=high)
            imag_part = jnp.einsum('pjk,jks->ps', u_row[0], block_imag, precision=high) + jnp.einsum('pjk,jks->ps', u_row[1], block_real, precision=high)
            return jnp.stack([real_part, imag_part]).astype(jnp.bfloat16)
        row_spectra = lax.map(one_row, (v_freq, u_freq, tile_ranks[slot]))
        spectra_list.append(jnp.moveaxis(row_spectra, 1, 0).reshape(2, NR, NS))
    spectra = lax.optimization_barrier(jnp.stack(spectra_list)).astype(jnp.float32)
    freq_index = jnp.arange(F, dtype=jnp.int32)
    weights = 1 + freq_index * (NT // 2 // F)
    times = jnp.arange(NT, dtype=jnp.int32)
    phase = (weights[:, None] * times[None, :] % NT).astype(jnp.float32) * (2.0 * math.pi / NT)
    scale = 1.0 / math.sqrt(2.0 * F)
    cos_basis = jnp.cos(phase) * scale
    sin_basis = -jnp.sin(phase) * scale
    high = lax.Precision.HIGHEST
    traces = jnp.einsum('fps,ft->pst', spectra[:, 0], cos_basis, precision=high) + jnp.einsum('fps,ft->pst', spectra[:, 1], sin_basis, precision=high)
    return jnp.where(times[None, None, :] >= mute_start[:, :, None], traces, 0.0)
```

```python
import math

import jax
import jax.numpy as jnp
import numpy as np
from jax import lax
from jax.experimental import pallas as pl
from jax.experimental.pallas import tpu as pltpu
from jax.sharding import PartitionSpec as P

NT = 128
MIB = 1024 * 1024


def params(vmem):
    return pltpu.CompilerParams(vmem_limit_bytes=vmem * MIB)


def lane_index(shape):
    return lax.broadcasted_iota(jnp.int32, shape, len(shape) - 1)


def row_index(shape):
    return lax.broadcasted_iota(jnp.int32, shape, len(shape) - 2)


def stack_sources(recorded_ref, stacked_ref):
    for f in range(2):
        real = recorded_ref[f, 0]
        imag = recorded_ref[f, 1]
        stacked_ref[f, 0:256, 0:128] = real
        stacked_ref[f, 256:512, 0:128] = -imag
        stacked_ref[f, 0:256, 128:256] = imag
        stacked_ref[f, 256:512, 128:256] = real


def transposed_dot(factors, stacked):
    return lax.dot_general(
        factors.reshape(512, 128),
        stacked,
        (((0,), (0,)), ((), ())),
        preferred_element_type=jnp.float32,
    )


def blocks_kernel(
    ranks_hbm, recorded_hbm, v_hbm, send_hbm,
    ranks, recorded, stacked, factors, blocks, small_sem, v_sem, send_sem,
):
    column = lax.axis_index("space")
    tile_count = factors.shape[1]
    parts = send_sem.shape[0]
    width = tile_count // parts
    get_ranks = pltpu.make_async_copy(ranks_hbm, ranks, small_sem.at[0])
    get_recorded = pltpu.make_async_copy(recorded_hbm, recorded, small_sem.at[1])
    get_ranks.start()
    get_recorded.start()

    def get_tile(f, i):
        return pltpu.make_async_copy(v_hbm.at[f, i], factors.at[f, i], v_sem.at[f, i])

    def get_first(f):
        first = pl.ds(0, width)
        return pltpu.make_async_copy(v_hbm.at[f, first], factors.at[f, first], v_sem.at[f, 0])

    def put_part(part):
        rows = pl.ds(part * width, width)
        return pltpu.make_async_copy(blocks.at[rows], send_hbm.at[rows], send_sem.at[part])

    for f in range(2):
        get_first(f).start()
    get_ranks.wait()

    @pl.loop(width, tile_count)
    def _(i):
        for f in range(2):

            @pl.when(ranks[tile_count * f + i, column] > 0)
            def _():
                get_tile(f, i).start()

    get_recorded.wait()
    stack_sources(recorded, stacked)
    row = row_index((64, 256))
    for part in range(parts):
        if part == 0:
            for f in range(2):
                get_first(f).wait()
        else:
            for i in range(part * width, (part + 1) * width):
                for f in range(2):

                    @pl.when(ranks[tile_count * f + i, column] > 0)
                    def _():
                        get_tile(f, i).wait()

        for i in range(part * width, (part + 1) * width):
            for f in range(2):
                product = transposed_dot(factors[f, i], stacked[f])[0:64]
                kept = row < ranks[tile_count * f + i, column]
                blocks[i, f * 64 : (f + 1) * 64] = jnp.where(kept, product, 0.0).astype(
                    jnp.bfloat16
                )
        put_part(part).start()
    for part in range(parts):
        put_part(part).wait()


def make_blocks(recorded, v_factors, ranks, parts=4):
    tile_count = v_factors.shape[1]
    return pl.pallas_call(
        blocks_kernel,
        in_specs=[pl.BlockSpec(memory_space=pl.ANY)] * 3,
        out_specs=pl.BlockSpec(memory_space=pltpu.HBM),
        out_shape=jax.ShapeDtypeStruct((tile_count, 128, 256), jnp.bfloat16),
        scratch_shapes=[
            pltpu.SMEM(ranks.shape, jnp.int32),
            pltpu.VMEM((2, 2, 256, 128), jnp.bfloat16),
            pltpu.VMEM((2, 512, 256), jnp.bfloat16),
            pltpu.VMEM((2, tile_count, 2, 256, 128), jnp.bfloat16),
            pltpu.VMEM((tile_count, 128, 256), jnp.bfloat16),
            pltpu.SemaphoreType.DMA((2,)),
            pltpu.SemaphoreType.DMA((2, tile_count)),
            pltpu.SemaphoreType.DMA((parts,)),
        ],
        compiler_params=params(60),
        cost_estimate=pl.CostEstimate(
            flops=4 * 10**9, bytes_accessed=11 * 10**6, transcendentals=0
        ),
        name="blocks",
    )(ranks, recorded, v_factors)


def own_kernel(ranks_hbm, recorded_ref, v_hbm, high_ref, ranks, factors, stacked, sem):
    column = lax.axis_index("space")
    get_ranks = pltpu.make_async_copy(ranks_hbm, ranks, sem.at[0])
    get_ranks.start()
    copies = [
        pltpu.make_async_copy(v_hbm.at[f, column], factors.at[f], sem.at[1 + f]) for f in range(2)
    ]
    for copy in copies:
        copy.start()
    stack_sources(recorded_ref, stacked)
    get_ranks.wait()
    row = row_index((64, 256)) + 64
    for f in range(2):
        copies[f].wait()
        product = transposed_dot(factors[f], stacked[f])[64:128]
        kept = row < ranks[ranks.shape[1] * f + column, column]
        high_ref[f * 64 : (f + 1) * 64] = jnp.where(kept, product, 0.0).astype(jnp.bfloat16)


def make_own(recorded, v_factors, ranks):
    return pl.pallas_call(
        own_kernel,
        in_specs=[
            pl.BlockSpec(memory_space=pl.ANY),
            pl.BlockSpec(memory_space=pltpu.VMEM),
            pl.BlockSpec(memory_space=pl.ANY),
        ],
        out_specs=pl.BlockSpec(memory_space=pltpu.VMEM),
        out_shape=jax.ShapeDtypeStruct((128, 256), jnp.bfloat16),
        scratch_shapes=[
            pltpu.SMEM(ranks.shape, jnp.int32),
            pltpu.VMEM((2, 2, 256, 128), jnp.bfloat16),
            pltpu.VMEM((2, 512, 256), jnp.bfloat16),
            pltpu.SemaphoreType.DMA((3,)),
        ],
        compiler_params=params(8),
        cost_estimate=pl.CostEstimate(
            flops=2 * 10**8, bytes_accessed=10**6, transcendentals=0
        ),
        name="own",
    )(ranks, recorded, v_factors)


def pack_kernel(u_ref, packed_ref, own_ref, wide_ref):
    rows = u_ref.shape[2]
    column = lax.axis_index("space")
    wide_ref[...] = u_ref[0, 0].reshape(rows * 32, 128).astype(jnp.float32)
    low_lanes = lane_index((rows, 128)) < 64
    for m in range(16):
        even = wide_ref[pl.ds(2 * m, rows, stride=32), :]
        odd = wide_ref[pl.ds(2 * m + 1, rows, stride=32), :]
        both = jnp.where(low_lanes, even, pltpu.roll(odd, 64, 1))
        packed_ref[0, :, m * 128 : (m + 1) * 128] = both.astype(jnp.bfloat16)
    own = wide_ref[pl.ds(column, rows, stride=32), :]
    own_ref[0] = pltpu.roll(own, 64, 1).astype(jnp.bfloat16)


def pack_factors(u_factors, rows=128):
    halves = 256 // rows
    return pl.pallas_call(
        pack_kernel,
        grid=(2, 2, halves),
        in_specs=[pl.BlockSpec((1, 1, rows, 32, 128), lambda f, c, h: (f, c, h, 0, 0))],
        out_specs=[
            pl.BlockSpec((1, rows, 2048), lambda f, c, h: (f, c * halves + h, 0)),
            pl.BlockSpec((1, rows, 128), lambda f, c, h: (f, c * halves + h, 0)),
        ],
        out_shape=[
            jax.ShapeDtypeStruct((2, 512, 2048), jnp.bfloat16),
            jax.ShapeDtypeStruct((2, 512, 128), jnp.bfloat16),
        ],
        scratch_shapes=[pltpu.VMEM((rows * 32, 128), jnp.float32)],
        compiler_params=params(16),
        cost_estimate=pl.CostEstimate(
            flops=10**6, bytes_accessed=40 * 10**6, transcendentals=0
        ),
        name="pack",
    )(u_factors)


def spectra_kernel(packed_ref, own_ref, received_ref, high_ref, *out_refs):
    group = lax.axis_index("freq")
    lane_part = lane_index((64, 128)) // 32
    for f in range(2):
        part = slice(f * 64, (f + 1) * 64)
        total = jnp.dot(
            packed_ref[f],
            received_ref[:, part, :].reshape(2048, 256),
            preferred_element_type=jnp.float32,
        ) + jnp.dot(own_ref[f, :, 0:64], high_ref[part], preferred_element_type=jnp.float32)
        real = total[0:256, 0:128] - total[256:512, 128:256]
        imag = total[0:256, 128:256] + total[256:512, 0:128]
        for c, value in enumerate((real, imag)):
            for m, out_ref in enumerate(out_refs):
                target = group ^ m
                message = jnp.zeros((64, 128), jnp.float32)
                for q in range(4):
                    moved = pltpu.roll(value[q * 64 : (q + 1) * 64], (q + 4 - target) % 4 * 32, 1)
                    message = jnp.where(lane_part == q, moved, message)
                out_ref[2 * f + c] = message.astype(jnp.bfloat16)


def make_spectra(packed, own, received, high):
    message = jax.ShapeDtypeStruct((4, 64, 128), jnp.bfloat16)
    return pl.pallas_call(
        spectra_kernel,
        in_specs=[pl.BlockSpec(memory_space=pltpu.VMEM)] * 4,
        out_specs=[pl.BlockSpec(memory_space=pltpu.VMEM)] * 4,
        out_shape=[message] * 4,
        compiler_params=params(16),
        cost_estimate=pl.CostEstimate(
            flops=2 * 10**9, bytes_accessed=7 * 10**6, transcendentals=0
        ),
        name="spectra",
    )(packed, own, received, high)


def traces_kernel(m0, m1, m2, m3, mute_ref, basis_ref, spread_ref, out_ref, left_ref, start_ref):
    step = pl.program_id(0)

    @pl.when(step == 0)
    def _():
        wide = jnp.concatenate([m[...].astype(jnp.float32) for m in (m0, m1, m2, m3)], axis=0)
        for r in range(8):
            part = wide[:, r * 8 : (r + 1) * 8].reshape(128, 128).T.astype(jnp.bfloat16)
            left_ref[r * 128 : (r + 1) * 128, 0:128] = part
            left_ref[r * 128 : (r + 1) * 128, 128:256] = part
            start = mute_ref[r * 8 : (r + 1) * 8, :].astype(jnp.float32)
            start = jnp.concatenate([start, jnp.zeros((120, 128), jnp.float32)], axis=0)
            start_ref[r * 128 : (r + 1) * 128, :] = start.T.astype(jnp.bfloat16)

    traces = jnp.dot(left_ref[...], basis_ref[...], preferred_element_type=jnp.float32)
    start = jnp.dot(start_ref[...], spread_ref[...], preferred_element_type=jnp.float32)
    times = lane_index((8, 4, 32, 128)).astype(jnp.float32)
    for p in range(2):
        lanes = slice(p * 128, (p + 1) * 128)
        value = traces[:, lanes].reshape(8, 4, 32, 128)
        kept = times >= start[:, lanes].reshape(8, 4, 32, 128)
        value = jnp.where(kept, value, 0.0)
        for q in range(4):
            out_ref[q, :, p] = value[:, q]


def make_traces(messages, mute, basis, spread):
    message = pl.BlockSpec((4, 64, 128), lambda s: (0, 0, 0))
    return pl.pallas_call(
        traces_kernel,
        grid=(4,),
        in_specs=[message] * 4
        + [
            pl.BlockSpec((64, 128), lambda s: (0, 0)),
            pl.BlockSpec((256, 256), lambda s: (0, s)),
            pl.BlockSpec((128, 256), lambda s: (0, s)),
        ],
        out_specs=pl.BlockSpec((4, 8, 2, 32, 128), lambda s: (0, 0, s, 0, 0)),
        out_shape=jax.ShapeDtypeStruct((4, 8, 8, 32, 128), jnp.float32),
        scratch_shapes=[
            pltpu.VMEM((1024, 256), jnp.bfloat16),
            pltpu.VMEM((1024, 128), jnp.bfloat16),
        ],
        compiler_params=params(32),
        cost_estimate=pl.CostEstimate(
            flops=2 * 10**9, bytes_accessed=6 * 10**6, transcendentals=0
        ),
        name="traces",
    )(*messages, mute, basis, spread)


def time_table(freq_total):
    weights = 1 + np.arange(freq_total) * (NT // 2 // freq_total)
    phase = (weights[:, None] * np.arange(NT)[None, :] % NT) * (2.0 * math.pi / NT)
    scale = 1.0 / math.sqrt(2.0 * freq_total)
    table = np.stack([np.cos(phase) * scale, -np.sin(phase) * scale], axis=1)
    return table.astype(np.float32)


def time_operands(group):
    table = time_table(8)
    top = table.astype(jnp.bfloat16)
    rest = (table - top.astype(np.float32)).astype(jnp.bfloat16)
    both = jnp.asarray(np.stack([top, rest])).reshape(2, 4, 4, NT)
    rows = jnp.take(both, group ^ jnp.arange(4, dtype=jnp.int32), axis=1).reshape(2, 16, NT)
    same = jnp.eye(8, dtype=jnp.bfloat16)
    basis = (rows[:, :, None, None, :] * same[None, None, :, :, None]).reshape(256, 8 * NT)
    spread = np.zeros((128, 8, NT), np.float32)
    for p in range(8):
        spread[p, p] = 1.0
    return basis, jnp.asarray(spread.reshape(128, 8 * NT), dtype=jnp.bfloat16)


def shards(recorded, v_factors, u_factors, tile_ranks, mute_start):
    ranks = tile_ranks.reshape(2 * tile_ranks.shape[1], tile_ranks.shape[2])
    send = make_blocks(recorded, v_factors, ranks)
    received = lax.all_to_all(send, "space", split_axis=0, concat_axis=0, tiled=True)
    high = make_own(recorded, v_factors, ranks)
    packed, own = pack_factors(u_factors)
    basis, spread = time_operands(lax.axis_index("freq"))
    mute = mute_start.reshape(4, 64, 32).transpose(1, 0, 2).reshape(64, 128)
    messages = make_spectra(packed, own, received, high)
    arrived = [messages[0]]
    for m in range(1, 4):
        pairs = [(z, z ^ m) for z in range(4)]
        arrived.append(lax.ppermute(messages[m], "freq", pairs))
    traces = make_traces(arrived, mute, basis, spread)
    return traces.reshape(256, 32, NT)


def solution(mesh):
    placed = (
        P("freq", None, "space", None),
        P("freq", None, None, "space", None),
        P("freq", None, "space", None, None),
        P("freq", None, None),
        P("space", "freq"),
    )
    return jax.shard_map(
        shards, mesh=mesh, in_specs=placed, out_specs=P("space", "freq", None), check_vma=False
    )
```

```python
import math

import jax
import jax.numpy as jnp
import numpy as np
from jax import lax
from jax.experimental import pallas as pl
from jax.experimental.pallas import tpu as pltpu
from jax.sharding import PartitionSpec as P

NT = 128
MIB = 1024 * 1024


def params(vmem):
    return pltpu.CompilerParams(vmem_limit_bytes=vmem * MIB)


def lane_index(shape):
    return lax.broadcasted_iota(jnp.int32, shape, len(shape) - 1)


def row_index(shape):
    return lax.broadcasted_iota(jnp.int32, shape, len(shape) - 2)


def stack_sources(recorded_ref, stacked_ref):
    for f in range(2):
        real = recorded_ref[f, 0]
        imag = recorded_ref[f, 1]
        stacked_ref[f, 0:256, 0:128] = real
        stacked_ref[f, 256:512, 0:128] = -imag
        stacked_ref[f, 0:256, 128:256] = imag
        stacked_ref[f, 256:512, 128:256] = real


def transposed_dot(factors, stacked):
    return lax.dot_general(
        factors.reshape(512, 128),
        stacked,
        (((0,), (0,)), ((), ())),
        preferred_element_type=jnp.float32,
    )


GROUP = 8


def order_tiles(order, rank_of, count):
    def place(i, n):
        some = rank_of(i) > 0
        order[jnp.where(some, n, count - 1 - (i - n))] = i
        return n + some.astype(jnp.int32)

    return lax.fori_loop(0, count, place, jnp.int32(0))


def blocks_kernel(
    ranks_hbm, recorded_hbm, v_hbm, send_hbm,
    ranks, order, recorded, stacked, factors, blocks, empty, small_sem, v_sem, send_sem,
):
    column = lax.axis_index("space")
    tile_count = factors.shape[1]
    get_ranks = pltpu.make_async_copy(ranks_hbm, ranks, small_sem.at[0])
    get_recorded = pltpu.make_async_copy(recorded_hbm, recorded, small_sem.at[1])
    get_ranks.start()
    get_recorded.start()
    empty[...] = jnp.zeros_like(empty)

    def get_tile(f, i):
        return pltpu.make_async_copy(v_hbm.at[f, i], factors.at[f, i], v_sem.at[f, i])

    def slot(f, i):
        return send_hbm.at[i, pl.ds(f * 64, 64)]

    def put_tile(f, i):
        return pltpu.make_async_copy(blocks.at[f, i], slot(f, i), send_sem.at[f])

    def put_empty(f, i):
        return pltpu.make_async_copy(empty, slot(f, i), send_sem.at[f])

    get_ranks.wait()
    counts = []
    for f in range(2):

        def rank_of(i, f=f):
            rank = ranks[tile_count * f + i, column]

            @pl.when(rank > 0)
            def _():
                get_tile(f, i).start()

            return rank

        counts.append(order_tiles(order.at[f], rank_of, tile_count))
    groups = [(n + GROUP - 1) // GROUP for n in counts]
    for f in range(2):

        @pl.loop(groups[f] * GROUP, tile_count)
        def _(n):
            put_empty(f, order[f, n]).start()

    get_recorded.wait()
    stack_sources(recorded, stacked)
    row = row_index((64, 256))
    for f in range(2):

        @pl.loop(0, groups[f])
        def _(g):
            tiles = [order[f, g * GROUP + t] for t in range(GROUP)]
            for t, i in enumerate(tiles):

                @pl.when(g * GROUP + t < counts[f])
                def _():
                    get_tile(f, i).wait()

            for i in tiles:
                product = transposed_dot(factors[f, i], stacked[f])[0:64]
                kept = row < ranks[tile_count * f + i, column]
                blocks[f, i] = jnp.where(kept, product, 0.0).astype(jnp.bfloat16)
            for i in tiles:
                put_tile(f, i).start()

    for f in range(2):

        @pl.loop(0, tile_count)
        def _(i):
            put_tile(f, i).wait()


def make_blocks(recorded, v_factors, ranks):
    tile_count = v_factors.shape[1]
    return pl.pallas_call(
        blocks_kernel,
        in_specs=[pl.BlockSpec(memory_space=pltpu.HBM)] * 3,
        out_specs=pl.BlockSpec(memory_space=pltpu.HBM),
        out_shape=jax.ShapeDtypeStruct((tile_count, 128, 256), jnp.bfloat16),
        scratch_shapes=[
            pltpu.SMEM(ranks.shape, jnp.int32),
            pltpu.SMEM((2, tile_count), jnp.int32),
            pltpu.VMEM((2, 2, 256, 128), jnp.bfloat16),
            pltpu.VMEM((2, 512, 256), jnp.bfloat16),
            pltpu.VMEM((2, tile_count, 2, 256, 128), jnp.bfloat16),
            pltpu.VMEM((2, tile_count, 64, 256), jnp.bfloat16),
            pltpu.VMEM((64, 256), jnp.bfloat16),
            pltpu.SemaphoreType.DMA((2,)),
            pltpu.SemaphoreType.DMA((2, tile_count)),
            pltpu.SemaphoreType.DMA((2,)),
        ],
        compiler_params=params(60),
        cost_estimate=pl.CostEstimate(
            flops=4 * 10**9, bytes_accessed=11 * 10**6, transcendentals=0
        ),
        name="blocks",
    )(ranks, recorded, v_factors)


def prepare_kernel(
    ranks_hbm, recorded_hbm, v_hbm, u_hbm, packed_ref, own_ref, high_ref,
    ranks, recorded, stacked, factors, rows_in, wide, small_sem, u_sem,
):
    column = lax.axis_index("space")
    tile_count = u_hbm.shape[3]
    count = rows_in.shape[1]
    steps = 1024 // count
    per_component = 256 // count

    def get_rows(step):
        f = step // (2 * per_component)
        c = step // per_component % 2
        rows = pl.ds(step % per_component * count, count)
        slot = step % 2
        return pltpu.make_async_copy(u_hbm.at[f, c, rows], rows_in.at[slot], u_sem.at[slot])

    get_rows(0).start()
    small = [
        pltpu.make_async_copy(ranks_hbm, ranks, small_sem.at[0]),
        pltpu.make_async_copy(recorded_hbm, recorded, small_sem.at[1]),
    ] + [
        pltpu.make_async_copy(v_hbm.at[f, column], factors.at[f], small_sem.at[2 + f])
        for f in range(2)
    ]
    for copy in small:
        copy.start()
    low_lanes = lane_index((count, 128)) < 64

    @pl.loop(0, steps)
    def _(step):
        @pl.when(step + 1 < steps)
        def _():
            get_rows(step + 1).start()

        get_rows(step).wait()
        wide[...] = rows_in[step % 2].reshape(count * tile_count, 128).astype(jnp.float32)
        f = step // (2 * per_component)
        rows = pl.ds(pl.multiple_of(step % (2 * per_component) * count, count), count)
        for m in range(tile_count // 2):
            even = wide[pl.ds(2 * m, count, stride=tile_count), :]
            odd = wide[pl.ds(2 * m + 1, count, stride=tile_count), :]
            both = jnp.where(low_lanes, even, pltpu.roll(odd, 64, 1))
            packed_ref[f, rows, m * 128 : (m + 1) * 128] = both.astype(jnp.bfloat16)
        own = wide[pl.ds(column, count, stride=tile_count), :]
        own_ref[f, rows, :] = pltpu.roll(own, 64, 1).astype(jnp.bfloat16)

    for copy in small:
        copy.wait()
    stack_sources(recorded, stacked)
    row = row_index((64, 256)) + 64
    for f in range(2):
        product = transposed_dot(factors[f], stacked[f])[64:128]
        kept = row < ranks[tile_count * f + column, column]
        high_ref[f * 64 : (f + 1) * 64] = jnp.where(kept, product, 0.0).astype(jnp.bfloat16)


def prepare(recorded, v_factors, u_factors, ranks, rows=128):
    tile_count = u_factors.shape[3]
    return pl.pallas_call(
        prepare_kernel,
        in_specs=[pl.BlockSpec(memory_space=pltpu.HBM)] * 4,
        out_specs=[pl.BlockSpec(memory_space=pltpu.VMEM)] * 3,
        out_shape=[
            jax.ShapeDtypeStruct((2, 512, tile_count * 64), jnp.bfloat16),
            jax.ShapeDtypeStruct((2, 512, 128), jnp.bfloat16),
            jax.ShapeDtypeStruct((128, 256), jnp.bfloat16),
        ],
        scratch_shapes=[
            pltpu.SMEM(ranks.shape, jnp.int32),
            pltpu.VMEM((2, 2, 256, 128), jnp.bfloat16),
            pltpu.VMEM((2, 512, 256), jnp.bfloat16),
            pltpu.VMEM((2, 2, 256, 128), jnp.bfloat16),
            pltpu.VMEM((2, rows, tile_count, 128), jnp.bfloat16),
            pltpu.VMEM((rows * tile_count, 128), jnp.float32),
            pltpu.SemaphoreType.DMA((4,)),
            pltpu.SemaphoreType.DMA((2,)),
        ],
        compiler_params=params(16),
        cost_estimate=pl.CostEstimate(
            flops=2 * 10**8, bytes_accessed=40 * 10**6, transcendentals=0
        ),
        name="prepare",
    )(ranks, recorded, v_factors, u_factors)


def spectra_kernel(packed_ref, own_ref, received_ref, high_ref, *out_refs):
    group = lax.axis_index("freq")
    lane_part = lane_index((64, 128)) // 32
    for f in range(2):
        part = slice(f * 64, (f + 1) * 64)
        total = jnp.dot(
            packed_ref[f],
            received_ref[:, part, :].reshape(2048, 256),
            preferred_element_type=jnp.float32,
        ) + jnp.dot(own_ref[f, :, 0:64], high_ref[part], preferred_element_type=jnp.float32)
        real = total[0:256, 0:128] - total[256:512, 128:256]
        imag = total[0:256, 128:256] + total[256:512, 0:128]
        for c, value in enumerate((real, imag)):
            for m, out_ref in enumerate(out_refs):
                target = group ^ m
                message = jnp.zeros((64, 128), jnp.float32)
                for q in range(4):
                    moved = pltpu.roll(value[q * 64 : (q + 1) * 64], (q + 4 - target) % 4 * 32, 1)
                    message = jnp.where(lane_part == q, moved, message)
                out_ref[2 * f + c] = message.astype(jnp.bfloat16)


def make_spectra(packed, own, received, high):
    message = jax.ShapeDtypeStruct((4, 64, 128), jnp.bfloat16)
    return pl.pallas_call(
        spectra_kernel,
        in_specs=[pl.BlockSpec(memory_space=pltpu.VMEM)] * 4,
        out_specs=[pl.BlockSpec(memory_space=pltpu.VMEM)] * 4,
        out_shape=[message] * 4,
        compiler_params=params(16),
        cost_estimate=pl.CostEstimate(
            flops=2 * 10**9, bytes_accessed=7 * 10**6, transcendentals=0
        ),
        name="spectra",
    )(packed, own, received, high)


def traces_kernel(m0, m1, m2, m3, mute_ref, basis_ref, spread_ref, out_ref, left_ref, start_ref):
    step = pl.program_id(0)

    @pl.when(step == 0)
    def _():
        wide = jnp.concatenate([m[...].astype(jnp.float32) for m in (m0, m1, m2, m3)], axis=0)
        for r in range(8):
            part = wide[:, r * 8 : (r + 1) * 8].reshape(128, 128).T.astype(jnp.bfloat16)
            left_ref[r * 128 : (r + 1) * 128, 0:128] = part
            left_ref[r * 128 : (r + 1) * 128, 128:256] = part
            start = mute_ref[r * 8 : (r + 1) * 8, :].astype(jnp.float32)
            start = jnp.concatenate([start, jnp.zeros((120, 128), jnp.float32)], axis=0)
            start_ref[r * 128 : (r + 1) * 128, :] = start.T.astype(jnp.bfloat16)

    traces = jnp.dot(left_ref[...], basis_ref[...], preferred_element_type=jnp.float32)
    start = jnp.dot(start_ref[...], spread_ref[...], preferred_element_type=jnp.float32)
    times = lane_index((8, 4, 32, 128)).astype(jnp.float32)
    for p in range(out_ref.shape[2]):
        lanes = slice(p * 128, (p + 1) * 128)
        value = traces[:, lanes].reshape(8, 4, 32, 128)
        kept = times >= start[:, lanes].reshape(8, 4, 32, 128)
        value = jnp.where(kept, value, 0.0)
        for q in range(4):
            out_ref[q, :, p] = value[:, q]


def make_traces(messages, mute, basis, spread, width=4):
    message = pl.BlockSpec((4, 64, 128), lambda s: (0, 0, 0))
    return pl.pallas_call(
        traces_kernel,
        grid=(8 // width,),
        in_specs=[message] * 4
        + [
            pl.BlockSpec((64, 128), lambda s: (0, 0)),
            pl.BlockSpec((256, width * NT), lambda s: (0, s)),
            pl.BlockSpec((128, width * NT), lambda s: (0, s)),
        ],
        out_specs=pl.BlockSpec((4, 8, width, 32, NT), lambda s: (0, 0, s, 0, 0)),
        out_shape=jax.ShapeDtypeStruct((4, 8, 8, 32, 128), jnp.float32),
        scratch_shapes=[
            pltpu.VMEM((1024, 256), jnp.bfloat16),
            pltpu.VMEM((1024, 128), jnp.bfloat16),
        ],
        compiler_params=params(32),
        cost_estimate=pl.CostEstimate(
            flops=2 * 10**9, bytes_accessed=6 * 10**6, transcendentals=0
        ),
        name="traces",
    )(*messages, mute, basis, spread)


def time_table(freq_total):
    weights = 1 + np.arange(freq_total) * (NT // 2 // freq_total)
    phase = (weights[:, None] * np.arange(NT)[None, :] % NT) * (2.0 * math.pi / NT)
    scale = 1.0 / math.sqrt(2.0 * freq_total)
    table = np.stack([np.cos(phase) * scale, -np.sin(phase) * scale], axis=1)
    return table.astype(np.float32)


def time_operands(group):
    table = time_table(8)
    top = table.astype(jnp.bfloat16)
    rest = (table - top.astype(np.float32)).astype(jnp.bfloat16)
    both = jnp.asarray(np.stack([top, rest])).reshape(2, 4, 4, NT)
    rows = jnp.take(both, group ^ jnp.arange(4, dtype=jnp.int32), axis=1).reshape(2, 16, NT)
    same = jnp.eye(8, dtype=jnp.bfloat16)
    basis = (rows[:, :, None, None, :] * same[None, None, :, :, None]).reshape(256, 8 * NT)
    spread = np.zeros((128, 8, NT), np.float32)
    for p in range(8):
        spread[p, p] = 1.0
    return basis, jnp.asarray(spread.reshape(128, 8 * NT), dtype=jnp.bfloat16)


def shards(recorded, v_factors, u_factors, tile_ranks, mute_start):
    ranks = tile_ranks.reshape(2 * tile_ranks.shape[1], tile_ranks.shape[2])
    send = make_blocks(recorded, v_factors, ranks)
    received = lax.all_to_all(send, "space", split_axis=0, concat_axis=0, tiled=True)
    packed, own, high = prepare(recorded, v_factors, u_factors, ranks)
    basis, spread = time_operands(lax.axis_index("freq"))
    mute = mute_start.reshape(4, 64, 32).transpose(1, 0, 2).reshape(64, 128)
    messages = make_spectra(packed, own, received, high)
    arrived = [messages[0]]
    for m in range(1, 4):
        pairs = [(z, z ^ m) for z in range(4)]
        arrived.append(lax.ppermute(messages[m], "freq", pairs))
    traces = make_traces(arrived, mute, basis, spread)
    return traces.reshape(256, 32, NT)


def solution(mesh):
    placed = (
        P("freq", None, "space", None),
        P("freq", None, None, "space", None),
        P("freq", None, "space", None, None),
        P("freq", None, None),
        P("space", "freq"),
    )
    return jax.shard_map(
        shards, mesh=mesh, in_specs=placed, out_specs=P("space", "freq", None), check_vma=False
    )
```

```python
import math

import jax
import jax.numpy as jnp
import numpy as np
from jax import lax
from jax.experimental import pallas as pl
from jax.experimental.pallas import tpu as pltpu
from jax.sharding import PartitionSpec as P

NT = 128
MIB = 1024 * 1024


def params(vmem):
    return pltpu.CompilerParams(vmem_limit_bytes=vmem * MIB)


def lane_index(shape):
    return lax.broadcasted_iota(jnp.int32, shape, len(shape) - 1)


def row_index(shape):
    return lax.broadcasted_iota(jnp.int32, shape, len(shape) - 2)


def stack_sources(recorded_ref, stacked_ref):
    for f in range(2):
        real = recorded_ref[f, 0]
        imag = recorded_ref[f, 1]
        stacked_ref[f, 0:256, 0:128] = real
        stacked_ref[f, 256:512, 0:128] = -imag
        stacked_ref[f, 0:256, 128:256] = imag
        stacked_ref[f, 256:512, 128:256] = real


def transposed_dot(factors, stacked):
    return lax.dot_general(
        factors.reshape(512, 128),
        stacked,
        (((0,), (0,)), ((), ())),
        preferred_element_type=jnp.float32,
    )


GROUP = 8


def order_tiles(order, rank_of, first, end):
    def place(i, n):
        some = rank_of(i) > 0
        order[jnp.where(some, n, end - 1 - (i - n))] = i
        return n + some.astype(jnp.int32)

    return lax.fori_loop(first, end, place, jnp.int32(0))


def blocks_kernel(
    ranks_hbm, recorded_hbm, v_hbm, send_hbm,
    ranks, order, recorded, stacked, factors, blocks, empty, small_sem, v_sem, send_sem,
):
    column = lax.axis_index("space")
    tile_count = factors.shape[1]
    get_ranks = pltpu.make_async_copy(ranks_hbm, ranks, small_sem.at[0])
    get_recorded = pltpu.make_async_copy(recorded_hbm, recorded, small_sem.at[1])
    def get_first(f):
        first = pl.ds(0, GROUP)
        return pltpu.make_async_copy(v_hbm.at[f, first], factors.at[f, first], v_sem.at[f, 0])

    get_ranks.start()
    get_recorded.start()
    for f in range(2):
        get_first(f).start()
    empty[...] = jnp.zeros_like(empty)

    def get_tile(f, i):
        return pltpu.make_async_copy(v_hbm.at[f, i], factors.at[f, i], v_sem.at[f, i])

    def slot(f, i):
        return send_hbm.at[i, pl.ds(f * 64, 64)]

    def put_tile(f, i):
        return pltpu.make_async_copy(blocks.at[f, i], slot(f, i), send_sem.at[f])

    def put_empty(f, i):
        return pltpu.make_async_copy(empty, slot(f, i), send_sem.at[f])

    get_ranks.wait()
    counts = []
    for f in range(2):

        def rank_of(i, f=f):
            rank = ranks[tile_count * f + i, column]

            @pl.when(rank > 0)
            def _():
                get_tile(f, i).start()

            return rank

        counts.append(order_tiles(order.at[f], rank_of, GROUP, tile_count))
    groups = [(n + GROUP - 1) // GROUP for n in counts]
    for f in range(2):

        @pl.loop(groups[f] * GROUP, tile_count - GROUP)
        def _(n):
            put_empty(f, order[f, n]).start()

    get_recorded.wait()
    stack_sources(recorded, stacked)
    row = row_index((64, 256))

    def multiply(f, tiles):
        for i in tiles:
            product = transposed_dot(factors[f, i], stacked[f])[0:64]
            kept = row < ranks[tile_count * f + i, column]
            blocks[f, i] = jnp.where(kept, product, 0.0).astype(jnp.bfloat16)
        for i in tiles:
            put_tile(f, i).start()

    for f in range(2):
        get_first(f).wait()
        multiply(f, range(GROUP))
    for f in range(2):

        @pl.loop(0, groups[f])
        def _(g):
            tiles = [order[f, g * GROUP + t] for t in range(GROUP)]
            for t, i in enumerate(tiles):

                @pl.when(g * GROUP + t < counts[f])
                def _():
                    get_tile(f, i).wait()

            multiply(f, tiles)

    for f in range(2):

        @pl.loop(0, tile_count)
        def _(i):
            put_tile(f, i).wait()


def make_blocks(recorded, v_factors, ranks):
    tile_count = v_factors.shape[1]
    return pl.pallas_call(
        blocks_kernel,
        in_specs=[pl.BlockSpec(memory_space=pltpu.HBM)] * 3,
        out_specs=pl.BlockSpec(memory_space=pltpu.HBM),
        out_shape=jax.ShapeDtypeStruct((tile_count, 128, 256), jnp.bfloat16),
        scratch_shapes=[
            pltpu.SMEM(ranks.shape, jnp.int32),
            pltpu.SMEM((2, tile_count), jnp.int32),
            pltpu.VMEM((2, 2, 256, 128), jnp.bfloat16),
            pltpu.VMEM((2, 512, 256), jnp.bfloat16),
            pltpu.VMEM((2, tile_count, 2, 256, 128), jnp.bfloat16),
            pltpu.VMEM((2, tile_count, 64, 256), jnp.bfloat16),
            pltpu.VMEM((64, 256), jnp.bfloat16),
            pltpu.SemaphoreType.DMA((2,)),
            pltpu.SemaphoreType.DMA((2, tile_count)),
            pltpu.SemaphoreType.DMA((2,)),
        ],
        compiler_params=params(60),
        cost_estimate=pl.CostEstimate(
            flops=4 * 10**9, bytes_accessed=11 * 10**6, transcendentals=0
        ),
        name="blocks",
    )(ranks, recorded, v_factors)


def prepare_kernel(
    ranks_hbm, recorded_hbm, v_hbm, u_hbm, packed_ref, own_ref, high_ref,
    ranks, recorded, stacked, factors, rows_in, wide, small_sem, u_sem,
):
    column = lax.axis_index("space")
    tile_count = u_hbm.shape[3]
    count = rows_in.shape[1]
    steps = 1024 // count
    per_component = 256 // count

    def get_rows(step):
        f = step // (2 * per_component)
        c = step // per_component % 2
        rows = pl.ds(step % per_component * count, count)
        slot = step % 2
        return pltpu.make_async_copy(u_hbm.at[f, c, rows], rows_in.at[slot], u_sem.at[slot])

    get_rows(0).start()
    small = [
        pltpu.make_async_copy(ranks_hbm, ranks, small_sem.at[0]),
        pltpu.make_async_copy(recorded_hbm, recorded, small_sem.at[1]),
    ] + [
        pltpu.make_async_copy(v_hbm.at[f, column], factors.at[f], small_sem.at[2 + f])
        for f in range(2)
    ]
    for copy in small:
        copy.start()
    low_lanes = lane_index((count, 128)) < 64

    @pl.loop(0, steps)
    def _(step):
        @pl.when(step + 1 < steps)
        def _():
            get_rows(step + 1).start()

        get_rows(step).wait()
        wide[...] = rows_in[step % 2].reshape(count * tile_count, 128).astype(jnp.float32)
        f = step // (2 * per_component)
        rows = pl.ds(pl.multiple_of(step % (2 * per_component) * count, count), count)
        for m in range(tile_count // 2):
            even = wide[pl.ds(2 * m, count, stride=tile_count), :]
            odd = wide[pl.ds(2 * m + 1, count, stride=tile_count), :]
            both = jnp.where(low_lanes, even, pltpu.roll(odd, 64, 1))
            packed_ref[f, rows, m * 128 : (m + 1) * 128] = both.astype(jnp.bfloat16)
        own = wide[pl.ds(column, count, stride=tile_count), :]
        own_ref[f, rows, :] = pltpu.roll(own, 64, 1).astype(jnp.bfloat16)

    for copy in small:
        copy.wait()
    stack_sources(recorded, stacked)
    row = row_index((64, 256)) + 64
    for f in range(2):
        product = transposed_dot(factors[f], stacked[f])[64:128]
        kept = row < ranks[tile_count * f + column, column]
        high_ref[f * 64 : (f + 1) * 64] = jnp.where(kept, product, 0.0).astype(jnp.bfloat16)


def prepare(recorded, v_factors, u_factors, ranks, rows=128):
    tile_count = u_factors.shape[3]
    return pl.pallas_call(
        prepare_kernel,
        in_specs=[pl.BlockSpec(memory_space=pltpu.HBM)] * 4,
        out_specs=[pl.BlockSpec(memory_space=pltpu.VMEM)] * 3,
        out_shape=[
            jax.ShapeDtypeStruct((2, 512, tile_count * 64), jnp.bfloat16),
            jax.ShapeDtypeStruct((2, 512, 128), jnp.bfloat16),
            jax.ShapeDtypeStruct((128, 256), jnp.bfloat16),
        ],
        scratch_shapes=[
            pltpu.SMEM(ranks.shape, jnp.int32),
            pltpu.VMEM((2, 2, 256, 128), jnp.bfloat16),
            pltpu.VMEM((2, 512, 256), jnp.bfloat16),
            pltpu.VMEM((2, 2, 256, 128), jnp.bfloat16),
            pltpu.VMEM((2, rows, tile_count, 128), jnp.bfloat16),
            pltpu.VMEM((rows * tile_count, 128), jnp.float32),
            pltpu.SemaphoreType.DMA((4,)),
            pltpu.SemaphoreType.DMA((2,)),
        ],
        compiler_params=params(50),
        cost_estimate=pl.CostEstimate(
            flops=2 * 10**8, bytes_accessed=40 * 10**6, transcendentals=0
        ),
        name="prepare",
    )(ranks, recorded, v_factors, u_factors)


def spectra_kernel(packed_ref, own_ref, received_ref, high_ref, *out_refs):
    group = lax.axis_index("freq")
    lane_part = lane_index((64, 128)) // 32
    for f in range(2):
        part = slice(f * 64, (f + 1) * 64)
        total = jnp.dot(
            packed_ref[f],
            received_ref[:, part, :].reshape(2048, 256),
            preferred_element_type=jnp.float32,
        ) + jnp.dot(own_ref[f, :, 0:64], high_ref[part], preferred_element_type=jnp.float32)
        real = total[0:256, 0:128] - total[256:512, 128:256]
        imag = total[0:256, 128:256] + total[256:512, 0:128]
        for c, value in enumerate((real, imag)):
            for m, out_ref in enumerate(out_refs):
                target = group ^ m
                message = jnp.zeros((64, 128), jnp.float32)
                for q in range(4):
                    moved = pltpu.roll(value[q * 64 : (q + 1) * 64], (q + 4 - target) % 4 * 32, 1)
                    message = jnp.where(lane_part == q, moved, message)
                out_ref[2 * f + c] = message.astype(jnp.bfloat16)


def make_spectra(packed, own, received, high):
    message = jax.ShapeDtypeStruct((4, 64, 128), jnp.bfloat16)
    return pl.pallas_call(
        spectra_kernel,
        in_specs=[pl.BlockSpec(memory_space=pltpu.VMEM)] * 4,
        out_specs=[pl.BlockSpec(memory_space=pltpu.VMEM)] * 4,
        out_shape=[message] * 4,
        compiler_params=params(16),
        cost_estimate=pl.CostEstimate(
            flops=2 * 10**9, bytes_accessed=7 * 10**6, transcendentals=0
        ),
        name="spectra",
    )(packed, own, received, high)


def traces_kernel(m0, m1, m2, m3, mute_ref, basis_ref, spread_ref, out_ref, left_ref, start_ref):
    step = pl.program_id(0)

    @pl.when(step == 0)
    def _():
        wide = jnp.concatenate([m[...].astype(jnp.float32) for m in (m0, m1, m2, m3)], axis=0)
        for r in range(8):
            part = wide[:, r * 8 : (r + 1) * 8].reshape(128, 128).T.astype(jnp.bfloat16)
            left_ref[r * 128 : (r + 1) * 128, 0:128] = part
            left_ref[r * 128 : (r + 1) * 128, 128:256] = part
            start = mute_ref[r * 8 : (r + 1) * 8, :].astype(jnp.float32)
            start = jnp.concatenate([start, jnp.zeros((120, 128), jnp.float32)], axis=0)
            start_ref[r * 128 : (r + 1) * 128, :] = start.T.astype(jnp.bfloat16)

    traces = jnp.dot(left_ref[...], basis_ref[...], preferred_element_type=jnp.float32)
    start = jnp.dot(start_ref[:, 0:16], spread_ref[...], preferred_element_type=jnp.float32)
    times = lane_index((8, 4, 32, 128)).astype(jnp.float32)
    for p in range(out_ref.shape[2]):
        lanes = slice(p * 128, (p + 1) * 128)
        value = traces[:, lanes].reshape(8, 4, 32, 128)
        kept = times >= start[:, lanes].reshape(8, 4, 32, 128)
        value = jnp.where(kept, value, 0.0)
        for q in range(4):
            out_ref[q, :, p] = value[:, q]


def make_traces(messages, mute, basis, spread, width=4):
    message = pl.BlockSpec((4, 64, 128), lambda s: (0, 0, 0))
    return pl.pallas_call(
        traces_kernel,
        grid=(8 // width,),
        in_specs=[message] * 4
        + [
            pl.BlockSpec((64, 128), lambda s: (0, 0)),
            pl.BlockSpec((256, width * NT), lambda s: (0, s)),
            pl.BlockSpec((16, width * NT), lambda s: (0, s)),
        ],
        out_specs=pl.BlockSpec((4, 8, width, 32, NT), lambda s: (0, 0, s, 0, 0)),
        out_shape=jax.ShapeDtypeStruct((4, 8, 8, 32, 128), jnp.float32),
        scratch_shapes=[
            pltpu.VMEM((1024, 256), jnp.bfloat16),
            pltpu.VMEM((1024, 128), jnp.bfloat16),
        ],
        compiler_params=params(32),
        cost_estimate=pl.CostEstimate(
            flops=2 * 10**9, bytes_accessed=6 * 10**6, transcendentals=0
        ),
        name="traces",
    )(*messages, mute, basis, spread)


def time_table(freq_total):
    weights = 1 + np.arange(freq_total) * (NT // 2 // freq_total)
    phase = (weights[:, None] * np.arange(NT)[None, :] % NT) * (2.0 * math.pi / NT)
    scale = 1.0 / math.sqrt(2.0 * freq_total)
    table = np.stack([np.cos(phase) * scale, -np.sin(phase) * scale], axis=1)
    return table.astype(np.float32)


def time_operands(group):
    table = time_table(8)
    top = table.astype(jnp.bfloat16)
    rest = (table - top.astype(np.float32)).astype(jnp.bfloat16)
    both = jnp.asarray(np.stack([top, rest])).reshape(2, 4, 4, NT)
    rows = jnp.take(both, group ^ jnp.arange(4, dtype=jnp.int32), axis=1).reshape(2, 16, NT)
    same = jnp.eye(8, dtype=jnp.bfloat16)
    basis = (rows[:, :, None, None, :] * same[None, None, :, :, None]).reshape(256, 8 * NT)
    spread = np.zeros((16, 8, NT), np.float32)
    for p in range(8):
        spread[p, p] = 1.0
    return basis, jnp.asarray(spread.reshape(16, 8 * NT), dtype=jnp.bfloat16)


def shards(recorded, v_factors, u_factors, tile_ranks, mute_start):
    ranks = tile_ranks.reshape(2 * tile_ranks.shape[1], tile_ranks.shape[2])
    send = make_blocks(recorded, v_factors, ranks)
    received = lax.all_to_all(send, "space", split_axis=0, concat_axis=0, tiled=True)
    packed, own, high = prepare(recorded, v_factors, u_factors, ranks)
    basis, spread = time_operands(lax.axis_index("freq"))
    mute = mute_start.reshape(4, 64, 32).transpose(1, 0, 2).reshape(64, 128)
    messages = make_spectra(packed, own, received, high)
    arrived = [messages[0]]
    for m in range(1, 4):
        pairs = [(z, z ^ m) for z in range(4)]
        arrived.append(lax.ppermute(messages[m], "freq", pairs))
    traces = make_traces(arrived, mute, basis, spread)
    return traces.reshape(256, 32, NT)


def solution(mesh):
    placed = (
        P("freq", None, "space", None),
        P("freq", None, None, "space", None),
        P("freq", None, "space", None, None),
        P("freq", None, None),
        P("space", "freq"),
    )
    return jax.shard_map(
        shards, mesh=mesh, in_specs=placed, out_specs=P("space", "freq", None), check_vma=False
    )
```
